1024 devices in a mesh: section: 16 (over y, core), dp: 64 (over x, z).
Axes of the slice: x: 8, y: 8, z: 8, core: 2. Of those that a mesh axis runs over, the one named last changes fastest.
Arguments:
- emb_rows: bfloat16 [65536, 7168], P('dp', 'section'), may hold values from -6 to 6
- grad_normed: bfloat16 [65536, 7168], P('dp', 'section'), may hold values from -6 to 6
- norm_gain: float32 [7168], P('section'), may hold values from 0.25 to 1.75
- owner_shard: int32 [65536, 1], P('dp'), may hold values from 0 to 63; in each aligned block of 1024 rows (0 to 1023, 1024 to 2047, ...) at most 24 rows name the same one
- row_in_shard: int32 [65536, 1], P('dp'), may hold values from 0 to 2019
Outputs:
- table_grad: bfloat16 [129280, 7168], P('dp', 'section')
- gain_gradient: float32 [7168], P('section')
The draws below stay inside these ranges and needn't reach their ends.
Inputs may be any that keep to these rules, and one draw needn't show every extreme that they name: `owner_shard`: among the rows of one device, at most 24 name any one shard, a bound that some block reaches.
All inputs are finite; a program needn't handle non-finite values.
Results may differ from the reference program's by a relative error of at most 0.0045.
Values may be sent and summed in bfloat16 or wider, within the bound.
No kernel may reach another device: no remote copies, remote signals or barrier semaphores. Data moves between devices by JAX's collectives and lax.ppermute only.
A program may use at most 32 MiB of HBM per device.

```python
import math
import jax
import jax.numpy as jnp
import numpy as np
from jax import lax

MODEL_WIDTH = 7168
VOCAB = 129280
TOK_DEV = 1024
TOKENS = 65536
CAP = 24
N_DP = 64


def plant(values, own_key, smallest, largest):
    longest = values.shape.index(max(values.shape))
    spots = []
    for shift in (0, 1):
        where = [jax.random.randint(jax.random.fold_in(own_key, axis), (), 0, length) for axis, length in enumerate(values.shape)]
        where[longest] = (where[longest] + shift) % values.shape[longest]
        spots.append(tuple(where))
    return values.at[spots[0]].set(smallest).at[spots[1]].set(largest)


def steps_of(key, dims, split, low, largest):
    gain, own = 1.0, jax.random.fold_in(key, 6)
    for axis_at, shards_of in split:
        draws = jnp.exp(jax.random.uniform(jax.random.fold_in(own, axis_at), (shards_of,), jnp.float32, low / len(split), largest / len(split)))
        gain = gain * jnp.repeat(draws, dims[axis_at] // shards_of).reshape([-1 if axis == axis_at else 1 for axis in range(len(dims))])
    return gain


def rank_bounds(amount, skew):
    portions = [(1 << 20) // math.isqrt(standing ** skew) + 1 for standing in range(1, amount + 1)]
    spread = 1 + sum(portions) // (1 << 30)
    return np.cumsum(np.array([max(1, weight // spread) for weight in portions]))


def skewed_ids(rng, shape, number_of, slope):
    listing = rank_bounds(number_of, slope)
    pick = jax.random.randint(jax.random.fold_in(rng, 1), shape, 0, int(listing[number_of - 1]))
    rank = jnp.searchsorted(jnp.asarray(listing, jnp.int32), pick, side="right")
    return jax.random.permutation(jax.random.fold_in(rng, 2), number_of)[rank].astype(jnp.int32)


def assign_block(stream_key, own, number, rows, amount, top, limit, slope):
    order = jax.random.permutation(stream_key, amount)
    crowded, common = portions_of(amount, rows * top, limit, slope, True), portions_of(amount, rows * top, limit, slope, False)
    places = jnp.arange(amount)

    def named(lengths, rotation):
        used = int((lengths > 0).sum())
        fixed = max(1, used // 4)
        shifted = fixed + (places - fixed + rotation * (used - fixed)) % max(1, amount - fixed)
        return jnp.zeros((amount,), jnp.int32).at[order[jnp.where(places < fixed, places, shifted)]].set(jnp.asarray(lengths, jnp.int32))

    lengths = jnp.where(number % 4 == 0, named(crowded, number // 4), named(common, number - number // 4 - 1))
    mixed = jax.random.permutation(jax.random.fold_in(own, 3), amount)
    donor, taker = mixed[0:amount // 2 * 2:2], mixed[1:amount // 2 * 2:2]
    margin = jnp.minimum(lengths[donor] - 1, limit - lengths[taker]) // 2
    margin = jnp.where((donor == order[0]) | (taker == order[0]) | (lengths[taker] == 0), 0, jnp.maximum(margin, 0))
    shifted = jax.random.randint(jax.random.fold_in(own, 4), (amount // 2,), 0, 1 << 20) % (margin + 1)
    lengths = lengths.at[donor].add(-shifted).at[taker].add(shifted)
    items = jnp.searchsorted(jnp.cumsum(lengths), jnp.arange(rows * top), side="right").astype(jnp.int32)
    table = items.reshape(top, rows).T
    table = table[jax.random.permutation(jax.random.fold_in(own, 1), rows)]
    rotation = jax.random.randint(jax.random.fold_in(own, 2), (rows, 1), 0, top)
    return jnp.take_along_axis(table, (jnp.arange(top)[None, :] + rotation) % top, axis=1)


def portions_of(count, total, bound, skew, full):
    portions = [(1 << 20) // math.isqrt(rank ** skew) + 1 for rank in range(1, count + 1)]
    largest = bound if full else min(bound, max(-(-total // count), total * portions[0] // sum(portions)))
    least = 1 if total - largest >= count - 1 else 0
    counts, surplus = [largest] + [least] * (count - 1), total - largest - least * (count - 1)
    while surplus > 0:
        free = [i for i in range(1, count) if counts[i] < largest] or [i for i in range(1, count) if counts[i] < bound]
        mass, left = sum([portions[i] for i in free]), surplus
        for i in free:
            extra = min(bound - counts[i], max(1, left * portions[i] // mass), surplus)
            counts[i] = counts[i] + extra
            surplus = surplus - extra
    return np.array(counts)


def scatter_about(stream_key, shape, width, reach, shards=(), kind=jnp.bfloat16):
    values = jax.random.normal(stream_key, shape, jnp.float32) * width
    if len(shards) > 0:
        values = steps_of(stream_key, shape, shards, -0.22, 0.18) * values
    return jnp.clip(values, min=-reach, max=reach).astype(kind)


def setup_inputs(seed: int = 0) -> dict:
    arg_keys = jax.random.split(jax.random.key(seed), 6)
    emb_rows = scatter_about(arg_keys[0], (TOKENS, MODEL_WIDTH), 1.0, 6.0, ((0, 64), (1, 16)))
    grad_normed = scatter_about(arg_keys[1], (TOKENS, MODEL_WIDTH), 1.0, 6.0, ((0, 64), (1, 16)))
    norm_gain = jnp.clip(1.0 + 0.15 * jax.random.normal(arg_keys[2], (MODEL_WIDTH,), jnp.float32), 0.25, 1.75)
    owner_shard_keys = jax.random.split(jax.random.fold_in(arg_keys[3], 1), TOKENS // TOK_DEV)
    owner_shard_turns = jax.random.permutation(jax.random.fold_in(arg_keys[3], 3), TOKENS // TOK_DEV)
    owner_shard = jax.vmap(lambda own, number: assign_block(jax.random.fold_in(arg_keys[3], 2), own, number, TOK_DEV, N_DP, 1, CAP, 2))(owner_shard_keys, owner_shard_turns).reshape((TOKENS, 1))
    row_in_shard = plant(skewed_ids(arg_keys[4], (TOKENS, 1), VOCAB // N_DP, 2), jax.random.fold_in(arg_keys[4], 3), 0, (VOCAB // N_DP) - 1).astype(jnp.int32)
    return dict(emb_rows=emb_rows, grad_normed=grad_normed, norm_gain=norm_gain, owner_shard=owner_shard, row_in_shard=row_in_shard)


EPS = 1e-06

def rows_backward(pair, norm_gain):
    emb_block, grad_block = pair
    embedding_rows = emb_block.astype(jnp.float32)
    output_gradient = grad_block.astype(jnp.float32)
    gained_gradient = norm_gain[None, :] * output_gradient
    sq = lax.optimization_barrier(jnp.sum(embedding_rows * embedding_rows, axis=1))
    inner_product = lax.optimization_barrier(jnp.sum(gained_gradient * embedding_rows, axis=1))
    inverse_norm = lax.rsqrt(sq / MODEL_WIDTH + EPS)
    normalized_rows = embedding_rows * inverse_norm[:, None]
    embedding_gradient = ((gained_gradient - normalized_rows * (inner_product * inverse_norm / MODEL_WIDTH)[:, None]) * inverse_norm[:, None]).astype(jnp.bfloat16)
    return (embedding_gradient, lax.optimization_barrier(jnp.sum(output_gradient * normalized_rows, axis=0)))

def reference(emb_rows, grad_normed, norm_gain, owner_shard, row_in_shard):
    block = math.gcd(TOKENS, 4096)
    count = TOKENS // block
    emb_b = emb_rows.reshape(count, block, MODEL_WIDTH)
    grad_b = grad_normed.reshape(count, block, MODEL_WIDTH)
    embedding_gradient, partial_gain = lax.map(lambda pair: rows_backward(pair, norm_gain), (emb_b, grad_b))
    gain_gradient = lax.optimization_barrier(jnp.sum(partial_gain, axis=0))
    ids = (owner_shard[:, 0] * (VOCAB // N_DP) + row_in_shard[:, 0]).astype(jnp.int32)
    table = jax.ops.segment_sum(embedding_gradient.reshape(TOKENS, MODEL_WIDTH).astype(jnp.float32), ids, num_segments=VOCAB)
    return (table.astype(jnp.bfloat16), gain_gradient)
```

```python
import jax
import jax.numpy as jnp
from jax import lax
from jax.experimental import pallas as pl
from jax.experimental.pallas import tpu as pltpu
from jax.sharding import PartitionSpec as P

MODEL_WIDTH = 7168
VOCAB = 129280
EPS = 1e-06
LANES = 128
STRIP = 16
PIECES = 3
GAP = 8
VMEM_LIMIT = 40 * 1024 * 1024


def iota(shape, dim):
    return lax.broadcasted_iota(jnp.int32, shape, dim)


def column_of(row):
    n = row.shape[1]
    return jnp.sum(jnp.where(iota((n, n), 0) == iota((n, n), 1), row, 0.0), axis=1, keepdims=True)


def fold_mask(n, width, first, lane_dim):
    shape = (n, LANES) if lane_dim == 1 else (LANES, n)
    lane = iota(shape, lane_dim) - first
    feature = iota(shape, 1 - lane_dim)
    hit = feature == lane
    for r in range(1, n // width):
        hit = hit | (feature - r * width == lane)
    return hit & (lane >= 0) & (lane < width)


def row_mask(n, width):
    offset = iota((8, n), 1) - iota((8, n), 0) * width
    return (offset >= 0) & (offset < width)


def stats_kernel(e_ref, dy_ref, gain_ref, out_ref):
    width, tokens = e_ref.shape
    gain = column_of(gain_ref[...])
    sq = jnp.zeros((8, tokens), jnp.float32)
    dot = jnp.zeros((8, tokens), jnp.float32)
    for k in range(0, width, STRIP):
        e = e_ref[k : k + STRIP, :].astype(jnp.float32)
        dy = dy_ref[k : k + STRIP, :].astype(jnp.float32)
        ee = e * e
        ed = e * (dy * gain[k : k + STRIP])
        sq = sq + ee[:8] + ee[8:]
        dot = dot + ed[:8] + ed[8:]
    sub = iota((8, LANES), 0)
    halves = []
    for total in (sq, dot):
        total = jnp.sum(total, axis=0, keepdims=True)
        tile = jnp.zeros((8, LANES), jnp.float32)
        for s in range(tokens // LANES):
            tile = jnp.where(sub == s, total[:, s * LANES : (s + 1) * LANES], tile)
        halves.append(tile)
    pair = jnp.concatenate(halves, axis=1)
    out_ref[...] = jnp.broadcast_to(pair[None], out_ref.shape)


def position_of(owner, shards, capacity):
    tokens = owner.shape[1]
    blocks = tokens // LANES
    marks = (iota((shards, tokens), 0) == owner).astype(jnp.float32)
    stacked = jnp.concatenate([marks[:, b * LANES : (b + 1) * LANES] for b in range(blocks)], axis=0)
    earlier = (iota((LANES, LANES), 0) < iota((LANES, LANES), 1)).astype(jnp.bfloat16)
    before = jnp.dot(stacked.astype(jnp.bfloat16), earlier, preferred_element_type=jnp.float32)
    totals = jnp.sum(stacked, axis=1, keepdims=True)
    start = jnp.zeros((shards, 1), jnp.float32)
    ranks = []
    for b in range(blocks):
        rows = slice(b * shards, (b + 1) * shards)
        ranks.append(jnp.sum(stacked[rows] * (before[rows] + start), axis=0, keepdims=True))
        start = start + totals[rows]
    rank = jnp.concatenate(ranks, axis=1)
    return owner * capacity + rank.astype(jnp.int32)


def rows_kernel(shards, capacity, e_ref, dy_ref, gain_ref, stats_ref, owner_ref, row_ref, out_ref, rows_ref, part_ref):
    width, tokens = e_ref.shape
    padded = out_ref.shape[1]
    gain = column_of(gain_ref[...])
    pair = jnp.sum(stats_ref[...], axis=0)
    sq = jnp.concatenate([pair[s : s + 1, :LANES] for s in range(8)], axis=1)
    dot = jnp.concatenate([pair[s : s + 1, LANES:] for s in range(8)], axis=1)
    rinv = lax.rsqrt(sq / MODEL_WIDTH + EPS)
    pull = dot * rinv * rinv / MODEL_WIDTH
    for k in range(0, width, STRIP):
        e = e_ref[k : k + STRIP, :].astype(jnp.float32)
        dy = dy_ref[k : k + STRIP, :].astype(jnp.float32)
        rows_ref[k : k + STRIP, :] = ((dy * gain[k : k + STRIP] - e * pull) * rinv).astype(jnp.bfloat16)
        term = dy * (e * rinv)
        part = term[:, :LANES]
        for s in range(1, tokens // LANES):
            part = part + term[:, s * LANES : (s + 1) * LANES]
        part_ref[k : k + STRIP, :] = part
    ids = row_ref[...]
    sub = iota((padded - width, tokens), 0)
    rows_ref[width:, :] = jnp.where(
        sub == 0, ids >> 3, jnp.where(sub == 1, ids & 7, 0)
    ).astype(jnp.float32).astype(jnp.bfloat16)
    span = padded - width - GAP
    first = LANES - span
    partial = jnp.sum(part_ref[...], axis=1, keepdims=True)
    spread = jnp.where(fold_mask(width, span, first, 1), partial, 0.0)
    fold = jnp.dot(
        row_mask(width, span).astype(jnp.float32), spread,
        precision=lax.Precision.HIGHEST, preferred_element_type=jnp.float32,
    )
    pieces = []
    for _ in range(PIECES):
        piece = fold.astype(jnp.bfloat16).astype(jnp.float32)
        pieces.append(piece)
        fold = fold - piece
    extra = jnp.concatenate(pieces, axis=0)
    position = position_of(owner_ref[...], shards, capacity)
    group = 8
    chunk = group * capacity
    rows = rows_ref[...]

    def step(i, carry):
        slot = iota((chunk, tokens), 0) + i * chunk
        pick = (slot == position).astype(jnp.float32).astype(jnp.bfloat16)
        got = lax.dot_general(pick, rows, (((1,), (1,)), ((), ())), preferred_element_type=jnp.float32)
        last = got[:, padded - LANES :].reshape(group, capacity, LANES) + extra[None]
        where = pl.ds(pl.multiple_of(i * chunk, chunk), chunk)
        out_ref[where, : padded - LANES] = got[:, : padded - LANES].astype(jnp.bfloat16)
        out_ref[where, padded - LANES :] = last.reshape(chunk, LANES).astype(jnp.bfloat16)
        return carry

    lax.fori_loop(0, shards // group, step, 0)


def table_kernel(capacity, width, got_ref, table_ref, gain_ref, turned_ref, id_ref):
    slots, padded = got_ref.shape
    tile = table_ref.shape[1]
    j = pl.program_id(0)

    @pl.when(j == 0)
    def _():
        turned_ref[...] = got_ref[...].T
        last = got_ref[:, padded - LANES :].astype(jnp.float32)
        lane = width - (padded - LANES)
        id_ref[...] = (last[:, lane : lane + 1] * 8.0 + last[:, lane + 1 : lane + 2]).astype(jnp.int32)
        total = jnp.sum(last.reshape(slots // capacity, capacity, LANES), axis=0)
        fold = total[:8] + total[8:16] + total[16:24]
        span = padded - width - GAP
        spread = jnp.dot(
            fold, fold_mask(width, span, LANES - span, 0).astype(jnp.float32),
            precision=lax.Precision.HIGHEST, preferred_element_type=jnp.float32,
        )
        gain_ref[...] = jnp.sum(jnp.where(row_mask(width, span), spread, 0.0), axis=0, keepdims=True)

    vocab = iota((slots, tile), 1) + j * tile
    onehot = (vocab == id_ref[...]).astype(jnp.float32).astype(jnp.bfloat16)
    table_ref[...] = jnp.dot(
        turned_ref[:width, :], onehot, preferred_element_type=jnp.float32
    ).astype(jnp.bfloat16)


def on_device(emb_rows, grad_normed, norm_gain, owner_shard, row_in_shard):
    tokens, width = emb_rows.shape
    sections, shards = lax.axis_size("section"), lax.axis_size("dp")
    capacity = 3 * tokens // (2 * shards)
    vocab_dev = VOCAB // shards
    padded = -(-width // LANES) * LANES
    slots = shards * capacity
    e, dy = emb_rows.T, grad_normed.T
    gain = norm_gain.reshape(1, width)
    owner, row = owner_shard.reshape(1, tokens), row_in_shard.reshape(1, tokens)
    params = pltpu.CompilerParams(vmem_limit_bytes=VMEM_LIMIT)
    stats = pl.pallas_call(
        stats_kernel,
        out_shape=jax.ShapeDtypeStruct((sections, 8, 2 * LANES), jnp.float32),
        compiler_params=params,
    )(e, dy, gain)
    stats = lax.all_to_all(stats, "section", 0, 0, tiled=True)
    message = pl.pallas_call(
        lambda *refs: rows_kernel(shards, capacity, *refs),
        out_shape=jax.ShapeDtypeStruct((slots, padded), jnp.bfloat16),
        scratch_shapes=[pltpu.VMEM((padded, tokens), jnp.bfloat16), pltpu.VMEM((width, LANES), jnp.float32)],
        compiler_params=params,
    )(e, dy, gain, stats, owner, row)
    got = lax.all_to_all(message.reshape(shards, capacity, padded), "dp", 0, 0, tiled=True)
    tile = 512
    table, gain_gradient = pl.pallas_call(
        lambda *refs: table_kernel(capacity, width, *refs),
        grid=(pl.cdiv(vocab_dev, tile),),
        in_specs=[pl.BlockSpec((slots, padded), lambda j: (0, 0))],
        out_specs=[pl.BlockSpec((width, tile), lambda j: (0, j)), pl.BlockSpec((1, width), lambda j: (0, 0))],
        out_shape=[
            jax.ShapeDtypeStruct((width, vocab_dev), jnp.bfloat16),
            jax.ShapeDtypeStruct((1, width), jnp.float32),
        ],
        scratch_shapes=[pltpu.VMEM((padded, slots), jnp.bfloat16), pltpu.VMEM((slots, 1), jnp.int32)],
        compiler_params=params,
    )(got.reshape(slots, padded))
    return (table.T, gain_gradient.reshape(width))


def solution(mesh):
    return jax.shard_map(
        on_device,
        mesh=mesh,
        in_specs=(
            P("dp", "section"),
            P("dp", "section"),
            P("section"),
            P("dp", None),
            P("dp", None),
        ),
        out_specs=(P("dp", "section"), P("section")),
        check_vma=False,
    )
```

```python
import jax
import jax.numpy as jnp
from jax import lax
from jax.experimental import pallas as pl
from jax.experimental.pallas import tpu as pltpu
from jax.sharding import PartitionSpec as P

MODEL_WIDTH = 7168
VOCAB = 129280
EPS = 1e-06
LANES = 128
STRIP = 16
PIECES = 3
GAP = 8
LOADS = 2
VMEM_LIMIT = 40 * 1024 * 1024
FULL_VMEM = 62 * 1024 * 1024
PICK = 16
TILE = 1024


def iota(shape, dim):
    return lax.broadcasted_iota(jnp.int32, shape, dim)


def column_of(row):
    n = row.shape[1]
    return jnp.sum(jnp.where(iota((n, n), 0) == iota((n, n), 1), row, 0.0), axis=1, keepdims=True)


def fold_mask(n, width, first, lane_dim):
    shape = (n, LANES) if lane_dim == 1 else (LANES, n)
    lane = iota(shape, lane_dim) - first
    feature = iota(shape, 1 - lane_dim)
    hit = feature == lane
    for r in range(1, n // width):
        hit = hit | (feature - r * width == lane)
    return hit & (lane >= 0) & (lane < width)


def row_mask(n, width):
    offset = iota((8, n), 1) - iota((8, n), 0) * width
    return (offset >= 0) & (offset < width)


def copies_of(pairs, sems, parts):
    out = []
    for p in range(parts):
        group = []
        for n, (source, target) in enumerate(pairs):
            rows = source.shape[0] // parts
            where = pl.ds(p * rows, rows)
            group.append(pltpu.make_async_copy(source.at[where], target.at[where], sems.at[p, n]))
        out.append(group)
    return out


def stats_kernel(e_hbm, dy_hbm, gain_hbm, out_ref, e_ref, dy_ref, gain_ref, sems, gain_sem):
    width, tokens = e_ref.shape
    gain_copy = pltpu.make_async_copy(gain_hbm, gain_ref, gain_sem)
    gain_copy.start()
    copies = copies_of([(e_hbm, e_ref), (dy_hbm, dy_ref)], sems, LOADS)
    for group in copies:
        for copy in group:
            copy.start()
    gain_copy.wait()
    gain = column_of(gain_ref[...])
    sq = jnp.zeros((8, tokens), jnp.float32)
    dot = jnp.zeros((8, tokens), jnp.float32)
    for p, group in enumerate(copies):
        for copy in group:
            copy.wait()
        for k in range(p * width // LOADS, (p + 1) * width // LOADS, STRIP):
            e = e_ref[k : k + STRIP, :].astype(jnp.float32)
            dy = dy_ref[k : k + STRIP, :].astype(jnp.float32)
            ee = e * e
            ed = e * (dy * gain[k : k + STRIP])
            sq = sq + ee[:8] + ee[8:]
            dot = dot + ed[:8] + ed[8:]
    sub = iota((8, LANES), 0)
    halves = []
    for total in (sq, dot):
        total = jnp.sum(total, axis=0, keepdims=True)
        tile = jnp.zeros((8, LANES), jnp.float32)
        for s in range(tokens // LANES):
            tile = jnp.where(sub == s, total[:, s * LANES : (s + 1) * LANES], tile)
        halves.append(tile)
    pair = jnp.concatenate(halves, axis=1)
    out_ref[...] = jnp.broadcast_to(pair[None], out_ref.shape)


def position_of(owner, shards, capacity):
    tokens = owner.shape[1]
    blocks = tokens // LANES
    marks = (iota((shards, tokens), 0) == owner).astype(jnp.float32)
    stacked = jnp.concatenate([marks[:, b * LANES : (b + 1) * LANES] for b in range(blocks)], axis=0)
    earlier = (iota((LANES, LANES), 0) < iota((LANES, LANES), 1)).astype(jnp.bfloat16)
    before = jnp.dot(stacked.astype(jnp.bfloat16), earlier, preferred_element_type=jnp.float32)
    totals = jnp.sum(stacked, axis=1, keepdims=True)
    start = jnp.zeros((shards, 1), jnp.float32)
    ranks = []
    for b in range(blocks):
        rows = slice(b * shards, (b + 1) * shards)
        ranks.append(jnp.sum(stacked[rows] * (before[rows] + start), axis=0, keepdims=True))
        start = start + totals[rows]
    rank = jnp.concatenate(ranks, axis=1)
    return owner * capacity + rank.astype(jnp.int32)


def rows_kernel(shards, capacity, e_ref, dy_ref, gain_ref, stats_ref, owner_ref, row_ref, out_ref, rows_ref, part_ref):
    width, tokens = e_ref.shape
    padded = out_ref.shape[1]
    position = position_of(owner_ref[...], shards, capacity)
    gain = column_of(gain_ref[...])
    pair = jnp.sum(stats_ref[...], axis=0)
    sq = jnp.concatenate([pair[s : s + 1, :LANES] for s in range(8)], axis=1)
    dot = jnp.concatenate([pair[s : s + 1, LANES:] for s in range(8)], axis=1)
    rinv = lax.rsqrt(sq / MODEL_WIDTH + EPS)
    pull = dot * rinv * rinv / MODEL_WIDTH
    for k in range(0, width, STRIP):
        e = e_ref[k : k + STRIP, :].astype(jnp.float32)
        dy = dy_ref[k : k + STRIP, :].astype(jnp.float32)
        rows_ref[k : k + STRIP, :] = ((dy * gain[k : k + STRIP] - e * pull) * rinv).astype(jnp.bfloat16)
        term = dy * (e * rinv)
        part = term[:, :LANES]
        for s in range(1, tokens // LANES):
            part = part + term[:, s * LANES : (s + 1) * LANES]
        part_ref[k : k + STRIP, :] = part
    ids = row_ref[...]
    sub = iota((padded - width, tokens), 0)
    rows_ref[width:, :] = jnp.where(
        sub == 0, ids >> 3, jnp.where(sub == 1, ids & 7, 0)
    ).astype(jnp.float32).astype(jnp.bfloat16)
    span = padded - width - GAP
    first = LANES - span
    partial = jnp.sum(part_ref[...], axis=1, keepdims=True)
    spread = jnp.where(fold_mask(width, span, first, 1), partial, 0.0)
    fold = jnp.dot(
        row_mask(width, span).astype(jnp.float32), spread,
        precision=lax.Precision.HIGHEST, preferred_element_type=jnp.float32,
    )
    pieces = []
    for _ in range(PIECES):
        piece = fold.astype(jnp.bfloat16).astype(jnp.float32)
        pieces.append(piece)
        fold = fold - piece
    extra = jnp.concatenate(pieces, axis=0)
    group = PICK
    chunk = group * capacity
    rows = rows_ref[...]

    def step(i, carry):
        half = chunk // 2
        pick = jnp.concatenate([onehot_rows(position, i * chunk + h * half, half) for h in range(2)], axis=0)
        got = lax.dot_general(pick, rows, (((1,), (1,)), ((), ())), preferred_element_type=jnp.float32)
        last = got[:, padded - LANES :].reshape(group, capacity, LANES) + extra[None]
        where = pl.ds(pl.multiple_of(i * chunk, chunk), chunk)
        out_ref[where, : padded - LANES] = got[:, : padded - LANES].astype(jnp.bfloat16)
        out_ref[where, padded - LANES :] = last.reshape(chunk, LANES).astype(jnp.bfloat16)
        return carry

    lax.fori_loop(0, shards // group, step, 0, unroll=True)


def onehot_rows(position, base, n):
    local = (position - base).astype(jnp.float32).astype(jnp.bfloat16)
    row = iota((n, position.shape[1]), 0).astype(jnp.float32).astype(jnp.bfloat16)
    return jnp.where(row == local, jnp.bfloat16(1), jnp.bfloat16(0))


def table_kernel(capacity, width, got_ref, table_ref, gain_ref, turned_ref, id_ref):
    slots, padded = got_ref.shape
    tile = table_ref.shape[1]
    j = pl.program_id(0)

    @pl.when(j == 0)
    def _():
        turned_ref[...] = got_ref[...].T
        last = got_ref[:, padded - LANES :].astype(jnp.float32)
        lane = width - (padded - LANES)
        ids = last[:, lane : lane + 1] * 8.0 + last[:, lane + 1 : lane + 2]
        id_ref[...] = jnp.broadcast_to(ids, id_ref.shape)
        total = jnp.sum(last.reshape(slots // capacity, capacity, LANES), axis=0)
        fold = total[:8] + total[8:16] + total[16:24]
        span = padded - width - GAP
        spread = jnp.dot(
            fold, fold_mask(width, span, LANES - span, 0).astype(jnp.float32),
            precision=lax.Precision.HIGHEST, preferred_element_type=jnp.float32,
        )
        gain_ref[...] = jnp.sum(jnp.where(row_mask(width, span), spread, 0.0), axis=0, keepdims=True)

    sub_tile = min(tile, 256)
    for t in range(tile // sub_tile):
        base = (j * tile + t * sub_tile).astype(jnp.float32)
        local = (id_ref[...] - base).astype(jnp.bfloat16)
        parts = []
        for q in range(sub_tile // LANES):
            lane = (iota((slots, LANES), 1) + q * LANES).astype(jnp.float32).astype(jnp.bfloat16)
            parts.append(jnp.where(local == lane, jnp.bfloat16(1), jnp.bfloat16(0)))
        onehot = jnp.concatenate(parts, axis=1)
        table_ref[:, t * sub_tile : (t + 1) * sub_tile] = jnp.dot(
            turned_ref[:width, :], onehot, preferred_element_type=jnp.float32
        ).astype(jnp.bfloat16)


def stats_call(e, dy, gain, sections):
    width, tokens = e.shape
    return pl.pallas_call(
        stats_kernel,
        in_specs=[pl.BlockSpec(memory_space=pltpu.HBM)] * 3,
        out_shape=jax.ShapeDtypeStruct((sections, 8, 2 * LANES), jnp.float32),
        scratch_shapes=[
            pltpu.VMEM((width, tokens), e.dtype),
            pltpu.VMEM((width, tokens), dy.dtype),
            pltpu.VMEM((1, width), jnp.float32),
            pltpu.SemaphoreType.DMA((LOADS, 2)),
            pltpu.SemaphoreType.DMA,
        ],
        compiler_params=pltpu.CompilerParams(vmem_limit_bytes=FULL_VMEM),
    )(e, dy, gain)


def rows_call(e, dy, gain, stats, owner, row, shards, capacity):
    width, tokens = e.shape
    padded = -(-width // LANES) * LANES
    return pl.pallas_call(
        lambda *refs: rows_kernel(shards, capacity, *refs),
        in_specs=[pl.BlockSpec(memory_space=pltpu.VMEM)] * 6,
        out_shape=jax.ShapeDtypeStruct((shards * capacity, padded), jnp.bfloat16),
        scratch_shapes=[
            pltpu.VMEM((padded, tokens), jnp.bfloat16),
            pltpu.VMEM((width, LANES), jnp.float32),
        ],
        compiler_params=pltpu.CompilerParams(vmem_limit_bytes=VMEM_LIMIT),
    )(e, dy, gain, stats, owner, row)


def table_call(got, capacity, width, vocab_dev):
    slots, padded = got.shape
    return pl.pallas_call(
        lambda *refs: table_kernel(capacity, width, *refs),
        grid=(pl.cdiv(vocab_dev, TILE),),
        in_specs=[pl.BlockSpec(memory_space=pltpu.VMEM)],
        out_specs=[pl.BlockSpec((width, TILE), lambda j: (0, j)), pl.BlockSpec((1, width), lambda j: (0, 0))],
        out_shape=[
            jax.ShapeDtypeStruct((width, vocab_dev), jnp.bfloat16),
            jax.ShapeDtypeStruct((1, width), jnp.float32),
        ],
        scratch_shapes=[pltpu.VMEM((padded, slots), jnp.bfloat16), pltpu.VMEM((slots, LANES), jnp.float32)],
        compiler_params=pltpu.CompilerParams(vmem_limit_bytes=VMEM_LIMIT),
    )(got)


def on_device(emb_rows, grad_normed, norm_gain, owner_shard, row_in_shard):
    tokens, width = emb_rows.shape
    sections, shards = lax.axis_size("section"), lax.axis_size("dp")
    capacity = 3 * tokens // (2 * shards)
    e, dy = emb_rows.T, grad_normed.T
    gain = norm_gain.reshape(1, width)
    owner, row = owner_shard.reshape(1, tokens), row_in_shard.reshape(1, tokens)
    stats = lax.all_to_all(stats_call(e, dy, gain, sections), "section", 0, 0, tiled=True)
    message = rows_call(e, dy, gain, stats, owner, row, shards, capacity)
    message = message.reshape(shards, capacity, -1)
    got = lax.all_to_all(message, "dp", 0, 0, tiled=True)
    table, gain_gradient = table_call(got.reshape(shards * capacity, -1), capacity, width, VOCAB // shards)
    return (table.T, gain_gradient.reshape(width))


def solution(mesh):
    return jax.shard_map(
        on_device,
        mesh=mesh,
        in_specs=(
            P("dp", "section"),
            P("dp", "section"),
            P("section"),
            P("dp", None),
            P("dp", None),
        ),
        out_specs=(P("dp", "section"), P("section")),
        check_vma=False,
    )
```

```python
import jax
import jax.numpy as jnp
from jax import lax
from jax.experimental import pallas as pl
from jax.experimental.pallas import tpu as pltpu
from jax.sharding import PartitionSpec as P

MODEL_WIDTH = 7168
VOCAB = 129280
EPS = 1e-06
LANES = 128
STRIP = 16
HALF = LANES // 2
LEVELS = 240 * 128
SCALE_LANE = HALF + 48
LOADS = 2
VMEM_LIMIT = 40 * 1024 * 1024
FULL_VMEM = 62 * 1024 * 1024
PICK = 16
TILE = 1024


def iota(shape, dim):
    return lax.broadcasted_iota(jnp.int32, shape, dim)


def column_of(row):
    n = row.shape[1]
    return jnp.sum(jnp.where(iota((n, n), 0) == iota((n, n), 1), row, 0.0), axis=1, keepdims=True)


def fold_mask(n, lane_dim):
    shape = (n, LANES) if lane_dim == 1 else (LANES, n)
    lane = iota(shape, lane_dim) - HALF
    feature = iota(shape, 1 - lane_dim)
    hit = feature == lane
    for r in range(1, n // HALF):
        hit = hit | (feature - r * HALF == lane)
    return hit & (lane >= 0)


def row_mask(n):
    offset = iota((8, n), 1) - (iota((8, n), 0) - 1) * HALF
    return (offset >= 0) & (offset < HALF)


def encode(q):
    size = jnp.abs(q)
    binade = jnp.floor(size * (1.0 / 128.0))
    value = 1.0 + (size - binade * 128.0) * (1.0 / 128.0)
    value = value * 2.0**-120
    for bit in (128, 64, 32, 16, 8, 4, 2, 1):
        take = binade >= bit
        binade = jnp.where(take, binade - bit, binade)
        for _ in range(2 if bit == 128 else 1):
            value = jnp.where(take, value * 2.0 ** min(bit, 64), value)
    return jnp.where(q < 0, -value, value)


def decode(code):
    value = jnp.abs(code)
    size = jnp.zeros_like(value)
    for bit in (128, 64, 32, 16, 8, 4, 2, 1):
        take = value >= 2.0 ** (bit - 120)
        size = jnp.where(take, size + bit * 128.0, size)
        for _ in range(2 if bit == 128 else 1):
            value = jnp.where(take, value * 2.0 ** -min(bit, 64), value)
    size = size + (value * 2.0**120 * 128.0 - 128.0)
    return jnp.where(code < 0, -size, size)


def copies_of(pairs, sems, parts):
    out = []
    for p in range(parts):
        group = []
        for n, (source, target) in enumerate(pairs):
            rows = source.shape[0] // parts
            where = pl.ds(p * rows, rows)
            group.append(pltpu.make_async_copy(source.at[where], target.at[where], sems.at[p, n]))
        out.append(group)
    return out


def stats_kernel(e_hbm, dy_hbm, gain_hbm, out_ref, e_ref, dy_ref, gain_ref, sems, gain_sem):
    width, tokens = e_ref.shape
    gain_copy = pltpu.make_async_copy(gain_hbm, gain_ref, gain_sem)
    gain_copy.start()
    copies = copies_of([(e_hbm, e_ref), (dy_hbm, dy_ref)], sems, LOADS)
    for group in copies:
        for copy in group:
            copy.start()
    gain_copy.wait()
    gain = column_of(gain_ref[...])
    sq = jnp.zeros((8, tokens), jnp.float32)
    dot = jnp.zeros((8, tokens), jnp.float32)
    for p, group in enumerate(copies):
        for copy in group:
            copy.wait()
        for k in range(p * width // LOADS, (p + 1) * width // LOADS, STRIP):
            e = e_ref[k : k + STRIP, :].astype(jnp.float32)
            dy = dy_ref[k : k + STRIP, :].astype(jnp.float32)
            ee = e * e
            ed = e * (dy * gain[k : k + STRIP])
            sq = sq + ee[:8] + ee[8:]
            dot = dot + ed[:8] + ed[8:]
    sub = iota((8, LANES), 0)
    halves = []
    for total in (sq, dot):
        total = jnp.sum(total, axis=0, keepdims=True)
        tile = jnp.zeros((8, LANES), jnp.float32)
        for s in range(tokens // LANES):
            tile = jnp.where(sub == s, total[:, s * LANES : (s + 1) * LANES], tile)
        halves.append(tile)
    pair = jnp.concatenate(halves, axis=1)
    out_ref[...] = jnp.broadcast_to(pair[None], out_ref.shape)


def ranks_of(owner, shards):
    tokens = owner.shape[1]
    blocks = tokens // LANES
    marks = (iota((shards, tokens), 0) == owner).astype(jnp.float32)
    stacked = jnp.concatenate([marks[:, b * LANES : (b + 1) * LANES] for b in range(blocks)], axis=0)
    earlier = (iota((LANES, LANES), 0) < iota((LANES, LANES), 1)).astype(jnp.bfloat16)
    before = jnp.dot(stacked.astype(jnp.bfloat16), earlier, preferred_element_type=jnp.float32)
    totals = jnp.sum(stacked, axis=1, keepdims=True)
    start = jnp.zeros((shards, 1), jnp.float32)
    ranks = []
    for b in range(blocks):
        rows = slice(b * shards, (b + 1) * shards)
        ranks.append(jnp.sum(stacked[rows] * (before[rows] + start), axis=0, keepdims=True))
        start = start + totals[rows]
    rank = jnp.concatenate(ranks, axis=1).astype(jnp.int32)
    return marks, rank


def rows_kernel(shards, capacity, e_ref, dy_ref, gain_ref, stats_ref, owner_ref, row_ref, out_ref, rows_ref, part_ref):
    width, tokens = e_ref.shape
    padded = rows_ref.shape[0]
    owner = owner_ref[...]
    marks, rank = ranks_of(owner, shards)
    position = owner * capacity + rank
    ids = row_ref[...]
    spot = iota((LANES, tokens), 0) - HALF
    id_rows = jnp.zeros((shards, LANES), jnp.float32)
    for part, first in ((ids >> 3, 0), (ids & 7, capacity)):
        id_rows = id_rows + lax.dot_general(
            (marks * part.astype(jnp.float32)).astype(jnp.bfloat16),
            (spot == rank + first).astype(jnp.float32).astype(jnp.bfloat16),
            (((1,), (1,)), ((), ())),
            preferred_element_type=jnp.float32,
        )
    gain = column_of(gain_ref[...])
    pair = jnp.sum(stats_ref[...], axis=0)
    sq = jnp.concatenate([pair[s : s + 1, :LANES] for s in range(8)], axis=1)
    dot = jnp.concatenate([pair[s : s + 1, LANES:] for s in range(8)], axis=1)
    rinv = lax.rsqrt(sq / MODEL_WIDTH + EPS)
    pull = dot * rinv * rinv / MODEL_WIDTH
    for k in range(0, width, STRIP):
        e = e_ref[k : k + STRIP, :].astype(jnp.float32)
        dy = dy_ref[k : k + STRIP, :].astype(jnp.float32)
        rows_ref[k : k + STRIP, :] = ((dy * gain[k : k + STRIP] - e * pull) * rinv).astype(jnp.bfloat16)
        term = dy * (e * rinv)
        part = term[:, :LANES]
        for s in range(1, tokens // LANES):
            part = part + term[:, s * LANES : (s + 1) * LANES]
        part_ref[k : k + STRIP, :] = part
    rows_ref[width:, :] = jnp.zeros((padded - width, tokens), jnp.bfloat16)
    partial = jnp.sum(part_ref[...], axis=1, keepdims=True)
    scale = jnp.maximum(jnp.max(jnp.abs(partial), axis=0, keepdims=True), 1e-30)
    steps = jnp.floor(partial * ((LEVELS - 1) / scale) + 0.5)
    steps = jnp.clip(steps, -(LEVELS - 1.0), LEVELS - 1.0)
    fold = jnp.dot(
        row_mask(width).astype(jnp.float32), jnp.where(fold_mask(width, 1), steps, 0.0),
        precision=lax.Precision.HIGHEST, preferred_element_type=jnp.float32,
    )
    sub, lane = iota((8, LANES), 0), iota((8, LANES), 1)
    extra = jnp.where((sub > 0) & (lane >= HALF), encode(jnp.floor(fold + 0.5)), 0.0)
    for n in range(3):
        piece = scale.astype(jnp.bfloat16).astype(jnp.float32)
        extra = jnp.where((sub == 0) & (lane == SCALE_LANE + n), piece, extra)
        scale = scale - piece
    rows = rows_ref[...]
    for first in range(0, shards, PICK):
        half = PICK // 2 * capacity
        pick = jnp.concatenate([onehot_rows(position, first * capacity + h * half, half) for h in range(2)], axis=0)
        got = lax.dot_general(pick, rows, (((1,), (1,)), ((), ())), preferred_element_type=jnp.float32)
        pieces = []
        for n in range(PICK):
            mine = got[n * capacity : (n + 1) * capacity]
            pieces += [mine[:, k : k + LANES] for k in range(0, padded - LANES, LANES)]
            last = mine[:, padded - LANES :]
            shard = first + n
            pieces.append(last[:8] + pltpu.roll(last[16:], HALF, 1))
            pieces.append(last[8:16] + jnp.where(sub == 0, extra + id_rows[shard : shard + 1], extra))
        size = out_ref.shape[0] // shards * PICK
        out_ref[first // PICK * size : (first // PICK + 1) * size] = jnp.concatenate(pieces, axis=0).astype(jnp.bfloat16)


def onehot_rows(position, base, n):
    local = (position - base).astype(jnp.float32).astype(jnp.bfloat16)
    row = iota((n, position.shape[1]), 0).astype(jnp.float32).astype(jnp.bfloat16)
    return jnp.where(row == local, jnp.bfloat16(1), jnp.bfloat16(0))


def table_kernel(shards, capacity, got_ref, table_ref, gain_ref, turned_ref, id_ref):
    width, tile = table_ref.shape
    slots = shards * capacity
    j = pl.program_id(0)

    @pl.when(j == 0)
    def _():
        got = got_ref[...].astype(jnp.float32).reshape(shards, -1, LANES)
        full = width // LANES
        for k in range(full):
            block = got[:, k * capacity : (k + 1) * capacity].reshape(slots, LANES)
            turned_ref[k * LANES : (k + 1) * LANES] = block.astype(jnp.bfloat16).T
        last = got[:, full * capacity :]
        block = jnp.concatenate([last, pltpu.roll(last[:, :8].reshape(shards * 8, LANES), HALF, 1).reshape(shards, 8, LANES)], axis=1)
        turned_ref[full * LANES :] = block.reshape(slots, LANES).astype(jnp.bfloat16).T[:HALF]
        extra = last[:, 8:]
        spot, lane = iota((capacity, LANES), 0), iota((capacity, LANES), 1) - HALF
        weight = jnp.where(lane == spot, 8.0, jnp.where(lane == spot + capacity, 1.0, 0.0))
        ids = jnp.sum(extra[:, :1] * weight[None], axis=2, keepdims=True).reshape(slots, 1)
        id_ref[...] = jnp.broadcast_to(ids, id_ref.shape)
        at = iota((1, LANES), 1)
        scale = jnp.where((at >= SCALE_LANE) & (at < SCALE_LANE + 3), extra[:, 0], 0.0)
        scale = jnp.sum(scale, axis=1, keepdims=True) * (1.0 / (LEVELS - 1))
        fold = jnp.sum(decode(extra) * scale[:, :, None], axis=0)
        spread = jnp.dot(
            fold, fold_mask(width, 0).astype(jnp.float32),
            precision=lax.Precision.HIGHEST, preferred_element_type=jnp.float32,
        )
        gain_ref[...] = jnp.sum(jnp.where(row_mask(width), spread, 0.0), axis=0, keepdims=True)

    sub_tile = min(tile, 256)
    for t in range(tile // sub_tile):
        base = (j * tile + t * sub_tile).astype(jnp.float32)
        local = (id_ref[...] - base).astype(jnp.bfloat16)
        parts = []
        for q in range(sub_tile // LANES):
            lane = (iota((slots, LANES), 1) + q * LANES).astype(jnp.float32).astype(jnp.bfloat16)
            parts.append(jnp.where(local == lane, jnp.bfloat16(1), jnp.bfloat16(0)))
        onehot = jnp.concatenate(parts, axis=1)
        table_ref[:, t * sub_tile : (t + 1) * sub_tile] = jnp.dot(
            turned_ref[...], onehot, preferred_element_type=jnp.float32
        ).astype(jnp.bfloat16)


def stats_call(e, dy, gain, sections):
    width, tokens = e.shape
    return pl.pallas_call(
        stats_kernel,
        in_specs=[pl.BlockSpec(memory_space=pltpu.HBM)] * 3,
        out_shape=jax.ShapeDtypeStruct((sections, 8, 2 * LANES), jnp.float32),
        scratch_shapes=[
            pltpu.VMEM((width, tokens), e.dtype),
            pltpu.VMEM((width, tokens), dy.dtype),
            pltpu.VMEM((1, width), jnp.float32),
            pltpu.SemaphoreType.DMA((LOADS, 2)),
            pltpu.SemaphoreType.DMA,
        ],
        compiler_params=pltpu.CompilerParams(vmem_limit_bytes=FULL_VMEM),
    )(e, dy, gain)


def rows_call(e, dy, gain, stats, owner, row, shards, capacity):
    width, tokens = e.shape
    padded = -(-width // LANES) * LANES
    message = width // LANES * capacity + 16
    return pl.pallas_call(
        lambda *refs: rows_kernel(shards, capacity, *refs),
        in_specs=[pl.BlockSpec(memory_space=pltpu.VMEM)] * 6,
        out_shape=jax.ShapeDtypeStruct((shards * message, LANES), jnp.bfloat16),
        scratch_shapes=[
            pltpu.VMEM((padded, tokens), jnp.bfloat16),
            pltpu.VMEM((width, LANES), jnp.float32),
        ],
        compiler_params=pltpu.CompilerParams(vmem_limit_bytes=VMEM_LIMIT),
    )(e, dy, gain, stats, owner, row)


def table_call(got, shards, capacity, width, vocab_dev):
    slots = shards * capacity
    return pl.pallas_call(
        lambda *refs: table_kernel(shards, capacity, *refs),
        grid=(pl.cdiv(vocab_dev, TILE),),
        in_specs=[pl.BlockSpec(memory_space=pltpu.VMEM)],
        out_specs=[pl.BlockSpec((width, TILE), lambda j: (0, j)), pl.BlockSpec((1, width), lambda j: (0, 0))],
        out_shape=[
            jax.ShapeDtypeStruct((width, vocab_dev), jnp.bfloat16),
            jax.ShapeDtypeStruct((1, width), jnp.float32),
        ],
        scratch_shapes=[pltpu.VMEM((width, slots), jnp.bfloat16), pltpu.VMEM((slots, LANES), jnp.float32)],
        compiler_params=pltpu.CompilerParams(vmem_limit_bytes=VMEM_LIMIT),
    )(got)


def on_device(emb_rows, grad_normed, norm_gain, owner_shard, row_in_shard):
    tokens, width = emb_rows.shape
    sections, shards = lax.axis_size("section"), lax.axis_size("dp")
    capacity = 3 * tokens // (2 * shards)
    e, dy = emb_rows.T, grad_normed.T
    gain = norm_gain.reshape(1, width)
    owner, row = owner_shard.reshape(1, tokens), row_in_shard.reshape(1, tokens)
    stats = lax.all_to_all(stats_call(e, dy, gain, sections), "section", 0, 0, tiled=True)
    message = rows_call(e, dy, gain, stats, owner, row, shards, capacity)
    message = message.reshape(shards, -1, LANES)
    got = lax.all_to_all(message, "dp", 0, 0, tiled=True)
    table, gain_gradient = table_call(got.reshape(-1, LANES), shards, capacity, width, VOCAB // shards)
    return (table.T, gain_gradient.reshape(width))


def solution(mesh):
    return jax.shard_map(
        on_device,
        mesh=mesh,
        in_specs=(
            P("dp", "section"),
            P("dp", "section"),
            P("section"),
            P("dp", None),
            P("dp", None),
        ),
        out_specs=(P("dp", "section"), P("section")),
        check_vma=False,
    )
```

```python
import jax
import jax.numpy as jnp
from jax import lax
from jax.experimental import pallas as pl
from jax.experimental.pallas import tpu as pltpu
from jax.sharding import PartitionSpec as P

MODEL_WIDTH = 7168
VOCAB = 129280
EPS = 1e-06
LANES = 128
STRIP = 16
HALF = LANES // 2
LEVELS = 240 * 128
SCALE_LANE = HALF + 48
LOADS = 2
VMEM_LIMIT = 40 * 1024 * 1024
FULL_VMEM = 62 * 1024 * 1024
PICK = 16
TILE = 1024


def iota(shape, dim):
    return lax.broadcasted_iota(jnp.int32, shape, dim)


def column_of(row):
    n = row.shape[1]
    return jnp.sum(jnp.where(iota((n, n), 0) == iota((n, n), 1), row, 0.0), axis=1, keepdims=True)


def fold_mask(n, lane_dim):
    shape = (n, LANES) if lane_dim == 1 else (LANES, n)
    lane = iota(shape, lane_dim) - HALF
    feature = iota(shape, 1 - lane_dim)
    hit = feature == lane
    for r in range(1, n // HALF):
        hit = hit | (feature - r * HALF == lane)
    return hit & (lane >= 0)


def row_mask(n):
    offset = iota((8, n), 1) - (iota((8, n), 0) - 1) * HALF
    return (offset >= 0) & (offset < HALF)


def encode(q):
    size = jnp.abs(q)
    binade = jnp.floor(size * (1.0 / 128.0))
    value = 1.0 + (size - binade * 128.0) * (1.0 / 128.0)
    value = value * 2.0**-120
    for bit in (128, 64, 32, 16, 8, 4, 2, 1):
        take = binade >= bit
        binade = jnp.where(take, binade - bit, binade)
        for _ in range(2 if bit == 128 else 1):
            value = jnp.where(take, value * 2.0 ** min(bit, 64), value)
    return jnp.where(q < 0, -value, value)


def decode(code):
    value = jnp.abs(code)
    size = jnp.zeros_like(value)
    for bit in (128, 64, 32, 16, 8, 4, 2, 1):
        take = value >= 2.0 ** (bit - 120)
        size = jnp.where(take, size + bit * 128.0, size)
        for _ in range(2 if bit == 128 else 1):
            value = jnp.where(take, value * 2.0 ** -min(bit, 64), value)
    size = size + (value * 2.0**120 * 128.0 - 128.0)
    return jnp.where(code < 0, -size, size)


def copies_of(pairs, sems, parts):
    out = []
    for p in range(parts):
        group = []
        for n, (source, target) in enumerate(pairs):
            rows = source.shape[0] // parts
            where = pl.ds(p * rows, rows)
            group.append(pltpu.make_async_copy(source.at[where], target.at[where], sems.at[p, n]))
        out.append(group)
    return out


def stats_kernel(e_hbm, dy_hbm, gain_hbm, out_ref, e_ref, dy_ref, gain_ref, sems, gain_sem):
    width, tokens = e_ref.shape
    gain_copy = pltpu.make_async_copy(gain_hbm, gain_ref, gain_sem)
    gain_copy.start()
    copies = copies_of([(e_hbm, e_ref), (dy_hbm, dy_ref)], sems, LOADS)
    for group in copies:
        for copy in group:
            copy.start()
    gain_copy.wait()
    gain = column_of(gain_ref[...])
    sq = jnp.zeros((8, tokens), jnp.float32)
    dot = jnp.zeros((8, tokens), jnp.float32)
    for p, group in enumerate(copies):
        for copy in group:
            copy.wait()
        for k in range(p * width // LOADS, (p + 1) * width // LOADS, STRIP):
            e = e_ref[k : k + STRIP, :].astype(jnp.float32)
            dy = dy_ref[k : k + STRIP, :].astype(jnp.float32)
            ee = e * e
            ed = e * (dy * gain[k : k + STRIP])
            sq = sq + ee[:8] + ee[8:]
            dot = dot + ed[:8] + ed[8:]
    sub = iota((8, LANES), 0)
    halves = []
    for total in (sq, dot):
        total = jnp.sum(total, axis=0, keepdims=True)
        tile = jnp.zeros((8, LANES), jnp.float32)
        for s in range(tokens // LANES):
            tile = jnp.where(sub == s, total[:, s * LANES : (s + 1) * LANES], tile)
        halves.append(tile)
    pair = jnp.concatenate(halves, axis=1)
    out_ref[...] = jnp.broadcast_to(pair[None], out_ref.shape)


def ranks_of(owner, shards):
    tokens = owner.shape[1]
    blocks = tokens // LANES
    marks = (iota((shards, tokens), 0) == owner).astype(jnp.float32)
    stacked = jnp.concatenate([marks[:, b * LANES : (b + 1) * LANES] for b in range(blocks)], axis=0)
    earlier = (iota((LANES, LANES), 0) < iota((LANES, LANES), 1)).astype(jnp.bfloat16)
    before = jnp.dot(stacked.astype(jnp.bfloat16), earlier, preferred_element_type=jnp.float32)
    totals = jnp.sum(stacked, axis=1, keepdims=True)
    start = jnp.zeros((shards, 1), jnp.float32)
    ranks = []
    for b in range(blocks):
        rows = slice(b * shards, (b + 1) * shards)
        ranks.append(jnp.sum(stacked[rows] * (before[rows] + start), axis=0, keepdims=True))
        start = start + totals[rows]
    rank = jnp.concatenate(ranks, axis=1).astype(jnp.int32)
    return marks, rank


def rows_kernel(shards, capacity, e_ref, dy_ref, gain_ref, stats_ref, owner_ref, row_ref, out_ref, rows_ref, part_ref):
    width, tokens = e_ref.shape
    padded = rows_ref.shape[0]
    owner = owner_ref[...]
    marks, rank = ranks_of(owner, shards)
    position = owner * capacity + rank
    ids = row_ref[...]
    spot = iota((LANES, tokens), 0) - HALF
    id_rows = jnp.zeros((shards, LANES), jnp.float32)
    for part, first in ((ids >> 3, 0), (ids & 7, capacity)):
        id_rows = id_rows + lax.dot_general(
            (marks * part.astype(jnp.float32)).astype(jnp.bfloat16),
            (spot == rank + first).astype(jnp.float32).astype(jnp.bfloat16),
            (((1,), (1,)), ((), ())),
            preferred_element_type=jnp.float32,
        )
    gain = column_of(gain_ref[...])
    pair = jnp.sum(stats_ref[...], axis=0)
    sq = jnp.concatenate([pair[s : s + 1, :LANES] for s in range(8)], axis=1)
    dot = jnp.concatenate([pair[s : s + 1, LANES:] for s in range(8)], axis=1)
    rinv = lax.rsqrt(sq / MODEL_WIDTH + EPS)
    pull = dot * rinv * rinv / MODEL_WIDTH
    for k in range(0, width, STRIP):
        e = e_ref[k : k + STRIP, :].astype(jnp.float32)
        dy = dy_ref[k : k + STRIP, :].astype(jnp.float32)
        rows_ref[k : k + STRIP, :] = ((dy * gain[k : k + STRIP] - e * pull) * rinv).astype(jnp.bfloat16)
        term = dy * (e * rinv)
        part = term[:, :LANES]
        for s in range(1, tokens // LANES):
            part = part + term[:, s * LANES : (s + 1) * LANES]
        part_ref[k : k + STRIP, :] = part
    rows_ref[width:, :] = jnp.zeros((padded - width, tokens), jnp.bfloat16)
    partial = jnp.sum(part_ref[...], axis=1, keepdims=True)
    scale = jnp.maximum(jnp.max(jnp.abs(partial), axis=0, keepdims=True), 1e-30)
    steps = jnp.floor(partial * ((LEVELS - 1) / scale) + 0.5)
    steps = jnp.clip(steps, -(LEVELS - 1.0), LEVELS - 1.0)
    fold = jnp.dot(
        row_mask(width).astype(jnp.float32), jnp.where(fold_mask(width, 1), steps, 0.0),
        precision=lax.Precision.HIGHEST, preferred_element_type=jnp.float32,
    )
    sub, lane = iota((8, LANES), 0), iota((8, LANES), 1)
    extra = jnp.where((sub > 0) & (lane >= HALF), encode(jnp.floor(fold + 0.5)), 0.0)
    for n in range(3):
        piece = scale.astype(jnp.bfloat16).astype(jnp.float32)
        extra = jnp.where((sub == 0) & (lane == SCALE_LANE + n), piece, extra)
        scale = scale - piece
    rows = rows_ref[...]
    for first in range(0, shards, PICK):
        half = PICK // 2 * capacity
        pick = jnp.concatenate([onehot_rows(position, first * capacity + h * half, half) for h in range(2)], axis=0)
        got = lax.dot_general(pick, rows, (((1,), (1,)), ((), ())), preferred_element_type=jnp.float32)
        pieces = []
        for n in range(PICK):
            mine = got[n * capacity : (n + 1) * capacity]
            pieces += [mine[:, k : k + LANES] for k in range(0, padded - LANES, LANES)]
            last = mine[:, padded - LANES :]
            shard = first + n
            pieces.append(last[:8] + pltpu.roll(last[16:], HALF, 1))
            pieces.append(last[8:16] + jnp.where(sub == 0, extra + id_rows[shard : shard + 1], extra))
        size = out_ref.shape[0] // shards * PICK
        out_ref[first // PICK * size : (first // PICK + 1) * size] = jnp.concatenate(pieces, axis=0).astype(jnp.bfloat16)


def onehot_rows(position, base, n):
    local = (position - base).astype(jnp.float32).astype(jnp.bfloat16)
    row = iota((n, position.shape[1]), 0).astype(jnp.float32).astype(jnp.bfloat16)
    return jnp.where(row == local, jnp.bfloat16(1), jnp.bfloat16(0))


def table_kernel(shards, capacity, got_ref, table_ref, gain_ref, turned_ref, id_ref):
    width, tile = table_ref.shape
    slots = shards * capacity
    j = pl.program_id(0)

    def sums():
        sub_tile = min(tile, 256)
        for t in range(tile // sub_tile):
            base = (j * tile + t * sub_tile).astype(jnp.float32)
            local = (id_ref[...] - base).astype(jnp.bfloat16)
            parts = []
            for q in range(sub_tile // LANES):
                lane = (iota((slots, LANES), 1) + q * LANES).astype(jnp.float32).astype(jnp.bfloat16)
                parts.append(jnp.where(local == lane, jnp.bfloat16(1), jnp.bfloat16(0)))
            onehot = jnp.concatenate(parts, axis=1)
            table_ref[:, t * sub_tile : (t + 1) * sub_tile] = jnp.dot(
                turned_ref[...], onehot, preferred_element_type=jnp.float32
            ).astype(jnp.bfloat16)

    @pl.when(j == 0)
    def _():
        got = got_ref[...].astype(jnp.float32).reshape(shards, -1, LANES)
        full = width // LANES
        for k in range(full):
            block = got[:, k * capacity : (k + 1) * capacity].reshape(slots, LANES)
            turned_ref[k * LANES : (k + 1) * LANES] = block.astype(jnp.bfloat16).T
        last = got[:, full * capacity :]
        block = jnp.concatenate([last, pltpu.roll(last[:, :8].reshape(shards * 8, LANES), HALF, 1).reshape(shards, 8, LANES)], axis=1)
        turned_ref[full * LANES :] = block.reshape(slots, LANES).astype(jnp.bfloat16).T[:HALF]
        extra = last[:, 8:]
        spot, lane = iota((capacity, LANES), 0), iota((capacity, LANES), 1) - HALF
        weight = jnp.where(lane == spot, 8.0, jnp.where(lane == spot + capacity, 1.0, 0.0))
        ids = jnp.sum(extra[:, :1] * weight[None], axis=2, keepdims=True).reshape(slots, 1)
        id_ref[...] = jnp.broadcast_to(ids, id_ref.shape)
        sums()
        at = iota((1, LANES), 1)
        scale = jnp.where((at >= SCALE_LANE) & (at < SCALE_LANE + 3), extra[:, 0], 0.0)
        scale = jnp.sum(scale, axis=1, keepdims=True) * (1.0 / (LEVELS - 1))
        fold = jnp.sum(decode(extra) * scale[:, :, None], axis=0)
        spread = jnp.dot(
            fold, fold_mask(width, 0).astype(jnp.float32),
            precision=lax.Precision.HIGHEST, preferred_element_type=jnp.float32,
        )
        gain_ref[...] = jnp.sum(jnp.where(row_mask(width), spread, 0.0), axis=0, keepdims=True)

    @pl.when(j > 0)
    def _():
        sums()


def stats_call(e, dy, gain, sections):
    width, tokens = e.shape
    return pl.pallas_call(
        stats_kernel,
        in_specs=[pl.BlockSpec(memory_space=pltpu.HBM)] * 3,
        out_shape=pltpu.VMEM((sections, 8, 2 * LANES), jnp.float32),
        scratch_shapes=[
            pltpu.VMEM((width, tokens), e.dtype),
            pltpu.VMEM((width, tokens), dy.dtype),
            pltpu.VMEM((1, width), jnp.float32),
            pltpu.SemaphoreType.DMA((LOADS, 2)),
            pltpu.SemaphoreType.DMA,
        ],
        compiler_params=pltpu.CompilerParams(vmem_limit_bytes=FULL_VMEM),
    )(e, dy, gain)


def rows_call(e, dy, gain, stats, owner, row, shards, capacity):
    width, tokens = e.shape
    padded = -(-width // LANES) * LANES
    message = width // LANES * capacity + 16
    return pl.pallas_call(
        lambda *refs: rows_kernel(shards, capacity, *refs),
        in_specs=[pl.BlockSpec(memory_space=pltpu.VMEM)] * 6,
        out_shape=jax.ShapeDtypeStruct((shards * message, LANES), jnp.bfloat16),
        scratch_shapes=[
            pltpu.VMEM((padded, tokens), jnp.bfloat16),
            pltpu.VMEM((width, LANES), jnp.float32),
        ],
        compiler_params=pltpu.CompilerParams(vmem_limit_bytes=VMEM_LIMIT),
    )(e, dy, gain, stats, owner, row)


def table_call(got, shards, capacity, width, vocab_dev):
    slots = shards * capacity
    return pl.pallas_call(
        lambda *refs: table_kernel(shards, capacity, *refs),
        grid=(pl.cdiv(vocab_dev, TILE),),
        in_specs=[pl.BlockSpec(memory_space=pltpu.VMEM)],
        out_specs=[pl.BlockSpec((width, TILE), lambda j: (0, j)), pl.BlockSpec((1, width), lambda j: (0, 0))],
        out_shape=[
            jax.ShapeDtypeStruct((width, vocab_dev), jnp.bfloat16),
            jax.ShapeDtypeStruct((1, width), jnp.float32),
        ],
        scratch_shapes=[pltpu.VMEM((width, slots), jnp.bfloat16), pltpu.VMEM((slots, LANES), jnp.float32)],
        compiler_params=pltpu.CompilerParams(vmem_limit_bytes=VMEM_LIMIT),
    )(got)


def on_device(emb_rows, grad_normed, norm_gain, owner_shard, row_in_shard):
    tokens, width = emb_rows.shape
    sections, shards = lax.axis_size("section"), lax.axis_size("dp")
    capacity = 3 * tokens // (2 * shards)
    e, dy = emb_rows.T, grad_normed.T
    gain = norm_gain.reshape(1, width)
    owner, row = owner_shard.reshape(1, tokens), row_in_shard.reshape(1, tokens)
    stats = lax.all_to_all(stats_call(e, dy, gain, sections), "section", 0, 0, tiled=True)
    message = rows_call(e, dy, gain, stats, owner, row, shards, capacity)
    message = message.reshape(shards, -1, LANES)
    got = lax.all_to_all(message, "dp", 0, 0, tiled=True)
    table, gain_gradient = table_call(got.reshape(-1, LANES), shards, capacity, width, VOCAB // shards)
    return (table.T, gain_gradient.reshape(width))


def solution(mesh):
    return jax.shard_map(
        on_device,
        mesh=mesh,
        in_specs=(
            P("dp", "section"),
            P("dp", "section"),
            P("section"),
            P("dp", None),
            P("dp", None),
        ),
        out_specs=(P("dp", "section"), P("section")),
        check_vma=False,
    )
```

```python
import math

import jax
import jax.numpy as jnp
from jax import lax
from jax.experimental import pallas as pl
from jax.experimental.pallas import tpu as pltpu
from jax.sharding import PartitionSpec as P

MODEL_WIDTH = 7168
VOCAB = 129280
EPS = 1e-06
LANES = 128
STRIP = 16
HALF = LANES // 2
LEVELS = 240 * 128
SCALE_LANE = HALF + 48
LOADS = 2
VMEM_LIMIT = 40 * 1024 * 1024
FULL_VMEM = 62 * 1024 * 1024
PICK = 16
TILE = 1024


def iota(shape, dim):
    return lax.broadcasted_iota(jnp.int32, shape, dim)


def column_of(row):
    n = row.shape[1]
    return jnp.sum(jnp.where(iota((n, n), 0) == iota((n, n), 1), row, 0.0), axis=1, keepdims=True)


def fold_mask(n, lane_dim):
    shape = (n, LANES) if lane_dim == 1 else (LANES, n)
    lane = iota(shape, lane_dim) - HALF
    feature = iota(shape, 1 - lane_dim)
    hit = feature == lane
    for r in range(1, n // HALF):
        hit = hit | (feature - r * HALF == lane)
    return hit & (lane >= 0)


def row_mask(n):
    offset = iota((8, n), 1) - (iota((8, n), 0) - 1) * HALF
    return (offset >= 0) & (offset < HALF)


def encode(q):
    size = jnp.abs(q)
    binade = jnp.floor(size * (1.0 / 128.0))
    value = 1.0 + (size - binade * 128.0) * (1.0 / 128.0)
    value = value * 2.0**-120
    for bit in (128, 64, 32, 16, 8, 4, 2, 1):
        take = binade >= bit
        binade = jnp.where(take, binade - bit, binade)
        for _ in range(2 if bit == 128 else 1):
            value = jnp.where(take, value * 2.0 ** min(bit, 64), value)
    return jnp.where(q < 0, -value, value)


def decode(code):
    value = jnp.abs(code)
    size = jnp.zeros_like(value)
    for bit in (128, 64, 32, 16, 8, 4, 2, 1):
        take = value >= 2.0 ** (bit - 120)
        size = jnp.where(take, size + bit * 128.0, size)
        for _ in range(2 if bit == 128 else 1):
            value = jnp.where(take, value * 2.0 ** -min(bit, 64), value)
    size = size + (value * 2.0**120 * 128.0 - 128.0)
    return jnp.where(code < 0, -size, size)


def copies_of(pairs, sems, parts):
    out = []
    for p in range(parts):
        group = []
        for n, (source, target) in enumerate(pairs):
            rows = source.shape[0] // parts
            where = pl.ds(p * rows, rows)
            group.append(pltpu.make_async_copy(source.at[where], target.at[where], sems.at[p, n]))
        out.append(group)
    return out


def stats_kernel(e_hbm, dy_hbm, gain_hbm, out_ref, e_ref, dy_ref, gain_ref, sems, gain_sem):
    width, tokens = e_ref.shape
    gain_copy = pltpu.make_async_copy(gain_hbm, gain_ref, gain_sem)
    gain_copy.start()
    copies = copies_of([(e_hbm, e_ref), (dy_hbm, dy_ref)], sems, LOADS)
    for group in copies:
        for copy in group:
            copy.start()
    gain_copy.wait()
    gain = column_of(gain_ref[...])
    sq = jnp.zeros((8, tokens), jnp.float32)
    dot = jnp.zeros((8, tokens), jnp.float32)
    for p, group in enumerate(copies):
        for copy in group:
            copy.wait()
        for k in range(p * width // LOADS, (p + 1) * width // LOADS, STRIP):
            e = e_ref[k : k + STRIP, :].astype(jnp.float32)
            dy = dy_ref[k : k + STRIP, :].astype(jnp.float32)
            ee = e * e
            ed = e * (dy * gain[k : k + STRIP])
            sq = sq + ee[:8] + ee[8:]
            dot = dot + ed[:8] + ed[8:]
    sub = iota((8, LANES), 0)
    halves = []
    for total in (sq, dot):
        total = jnp.sum(total, axis=0, keepdims=True)
        tile = jnp.zeros((8, LANES), jnp.float32)
        for s in range(tokens // LANES):
            tile = jnp.where(sub == s, total[:, s * LANES : (s + 1) * LANES], tile)
        halves.append(tile)
    pair = jnp.concatenate(halves, axis=1)
    out_ref[...] = jnp.broadcast_to(pair[None], out_ref.shape)


def ranks_of(owner, shards):
    tokens = owner.shape[1]
    blocks = tokens // LANES
    marks = (iota((shards, tokens), 0) == owner).astype(jnp.float32)
    stacked = jnp.concatenate([marks[:, b * LANES : (b + 1) * LANES] for b in range(blocks)], axis=0)
    earlier = (iota((LANES, LANES), 0) < iota((LANES, LANES), 1)).astype(jnp.bfloat16)
    before = jnp.dot(stacked.astype(jnp.bfloat16), earlier, preferred_element_type=jnp.float32)
    totals = jnp.sum(stacked, axis=1, keepdims=True)
    start = jnp.zeros((shards, 1), jnp.float32)
    ranks = []
    for b in range(blocks):
        rows = slice(b * shards, (b + 1) * shards)
        ranks.append(jnp.sum(stacked[rows] * (before[rows] + start), axis=0, keepdims=True))
        start = start + totals[rows]
    rank = jnp.concatenate(ranks, axis=1).astype(jnp.int32)
    return marks, rank


def rows_kernel(shards, capacity, e_ref, dy_ref, gain_ref, stats_ref, owner_ref, row_ref, out_ref, rows_ref, part_ref):
    width, tokens = e_ref.shape
    padded = rows_ref.shape[0]
    owner = owner_ref[...]
    marks, rank = ranks_of(owner, shards)
    side = math.isqrt(shards)
    line = lax.div(owner, side)
    place = lax.rem(lax.rem(owner, side) - line + side, side) * side + line
    position = place * capacity + rank
    ids = row_ref[...]
    spot = iota((LANES, tokens), 0) - HALF
    id_rows = jnp.zeros((shards, LANES), jnp.float32)
    for part, first in ((ids >> 3, 0), (ids & 7, capacity)):
        id_rows = id_rows + lax.dot_general(
            (marks * part.astype(jnp.float32)).astype(jnp.bfloat16),
            (spot == rank + first).astype(jnp.float32).astype(jnp.bfloat16),
            (((1,), (1,)), ((), ())),
            preferred_element_type=jnp.float32,
        )
    gain = column_of(gain_ref[...])
    pair = jnp.sum(stats_ref[...], axis=0)
    sq = jnp.concatenate([pair[s : s + 1, :LANES] for s in range(8)], axis=1)
    dot = jnp.concatenate([pair[s : s + 1, LANES:] for s in range(8)], axis=1)
    rinv = lax.rsqrt(sq / MODEL_WIDTH + EPS)
    pull = dot * rinv * rinv / MODEL_WIDTH
    for k in range(0, width, STRIP):
        e = e_ref[k : k + STRIP, :].astype(jnp.float32)
        dy = dy_ref[k : k + STRIP, :].astype(jnp.float32)
        rows_ref[k : k + STRIP, :] = ((dy * gain[k : k + STRIP] - e * pull) * rinv).astype(jnp.bfloat16)
        term = dy * (e * rinv)
        part = term[:, :LANES]
        for s in range(1, tokens // LANES):
            part = part + term[:, s * LANES : (s + 1) * LANES]
        part_ref[k : k + STRIP, :] = part
    rows_ref[width:, :] = jnp.zeros((padded - width, tokens), jnp.bfloat16)
    partial = jnp.sum(part_ref[...], axis=1, keepdims=True)
    scale = jnp.maximum(jnp.max(jnp.abs(partial), axis=0, keepdims=True), 1e-30)
    steps = jnp.floor(partial * ((LEVELS - 1) / scale) + 0.5)
    steps = jnp.clip(steps, -(LEVELS - 1.0), LEVELS - 1.0)
    high = jnp.floor(steps * (1.0 / 128.0))
    spots, lines = fold_mask(width, 1), row_mask(width).astype(jnp.float32).astype(jnp.bfloat16)
    fold = jnp.zeros((8, LANES), jnp.float32)
    for part, unit in ((high, 128.0), (steps - high * 128.0, 1.0)):
        spread = jnp.where(spots, part, 0.0).astype(jnp.bfloat16)
        fold = fold + unit * jnp.dot(lines, spread, preferred_element_type=jnp.float32)
    sub, lane = iota((8, LANES), 0), iota((8, LANES), 1)
    extra = jnp.where((sub > 0) & (lane >= HALF), encode(fold), 0.0)
    for n in range(3):
        piece = scale.astype(jnp.bfloat16).astype(jnp.float32)
        extra = jnp.where((sub == 0) & (lane == SCALE_LANE + n), piece, extra)
        scale = scale - piece
    rows = rows_ref[...]
    for first in range(0, shards, PICK):
        half = PICK // 2 * capacity
        pick = jnp.concatenate([onehot_rows(position, first * capacity + h * half, half) for h in range(2)], axis=0)
        got = lax.dot_general(pick, rows, (((1,), (1,)), ((), ())), preferred_element_type=jnp.float32)
        pieces = []
        for n in range(PICK):
            mine = got[n * capacity : (n + 1) * capacity]
            pieces += [mine[:, k : k + LANES] for k in range(0, padded - LANES, LANES)]
            last = mine[:, padded - LANES :]
            place = first + n
            shard = place % side * side + (place % side + place // side) % side
            pieces.append(last[:8] + pltpu.roll(last[16:], HALF, 1))
            pieces.append(last[8:16] + jnp.where(sub == 0, extra + id_rows[shard : shard + 1], extra))
        size = out_ref.shape[0] // shards * PICK
        out_ref[first // PICK * size : (first // PICK + 1) * size] = jnp.concatenate(pieces, axis=0).astype(jnp.bfloat16)


def onehot_rows(position, base, n):
    local = (position - base).astype(jnp.float32).astype(jnp.bfloat16)
    row = iota((n, position.shape[1]), 0).astype(jnp.float32).astype(jnp.bfloat16)
    return jnp.where(row == local, jnp.bfloat16(1), jnp.bfloat16(0))


def table_kernel(shards, capacity, got_ref, table_ref, gain_ref, turned_ref, id_ref):
    width, tile = table_ref.shape
    slots = shards * capacity
    j = pl.program_id(0)

    def sums():
        sub_tile = min(tile, 256)
        for t in range(tile // sub_tile):
            base = (j * tile + t * sub_tile).astype(jnp.float32)
            local = (id_ref[...] - base).astype(jnp.bfloat16)
            parts = []
            for q in range(sub_tile // LANES):
                lane = (iota((slots, LANES), 1) + q * LANES).astype(jnp.float32).astype(jnp.bfloat16)
                parts.append(jnp.where(local == lane, jnp.bfloat16(1), jnp.bfloat16(0)))
            onehot = jnp.concatenate(parts, axis=1)
            table_ref[:, t * sub_tile : (t + 1) * sub_tile] = jnp.dot(
                turned_ref[...], onehot, preferred_element_type=jnp.float32
            ).astype(jnp.bfloat16)

    @pl.when(j == 0)
    def _():
        got = got_ref[...].astype(jnp.float32).reshape(shards, -1, LANES)
        full = width // LANES
        for k in range(full):
            block = got[:, k * capacity : (k + 1) * capacity].reshape(slots, LANES)
            turned_ref[k * LANES : (k + 1) * LANES] = block.astype(jnp.bfloat16).T
        last = got[:, full * capacity :]
        block = jnp.concatenate([last, pltpu.roll(last[:, :8].reshape(shards * 8, LANES), HALF, 1).reshape(shards, 8, LANES)], axis=1)
        turned_ref[full * LANES :] = block.reshape(slots, LANES).astype(jnp.bfloat16).T[:HALF]
        extra = last[:, 8:]
        spot, lane = iota((capacity, LANES), 0), iota((capacity, LANES), 1) - HALF
        weight = jnp.where(lane == spot, 8.0, jnp.where(lane == spot + capacity, 1.0, 0.0))
        ids = jnp.sum(extra[:, :1] * weight[None], axis=2, keepdims=True).reshape(slots, 1)
        id_ref[...] = jnp.broadcast_to(ids, id_ref.shape)
        sums()
        at = iota((1, LANES), 1)
        scale = jnp.where((at >= SCALE_LANE) & (at < SCALE_LANE + 3), extra[:, 0], 0.0)
        scale = jnp.sum(scale, axis=1, keepdims=True) * (1.0 / (LEVELS - 1))
        fold = jnp.sum(decode(extra) * scale[:, :, None], axis=0)
        spread = jnp.dot(
            fold, fold_mask(width, 0).astype(jnp.float32),
            precision=lax.Precision.HIGHEST, preferred_element_type=jnp.float32,
        )
        gain_ref[...] = jnp.sum(jnp.where(row_mask(width), spread, 0.0), axis=0, keepdims=True)

    @pl.when(j > 0)
    def _():
        sums()


def stats_call(e, dy, gain, sections):
    width, tokens = e.shape
    return pl.pallas_call(
        stats_kernel,
        in_specs=[pl.BlockSpec(memory_space=pltpu.HBM)] * 3,
        out_shape=pltpu.VMEM((sections, 8, 2 * LANES), jnp.float32),
        scratch_shapes=[
            pltpu.VMEM((width, tokens), e.dtype),
            pltpu.VMEM((width, tokens), dy.dtype),
            pltpu.VMEM((1, width), jnp.float32),
            pltpu.SemaphoreType.DMA((LOADS, 2)),
            pltpu.SemaphoreType.DMA,
        ],
        compiler_params=pltpu.CompilerParams(vmem_limit_bytes=FULL_VMEM),
    )(e, dy, gain)


def rows_call(e, dy, gain, stats, owner, row, shards, capacity):
    width, tokens = e.shape
    padded = -(-width // LANES) * LANES
    message = width // LANES * capacity + 16
    return pl.pallas_call(
        lambda *refs: rows_kernel(shards, capacity, *refs),
        in_specs=[pl.BlockSpec(memory_space=pltpu.VMEM)] * 6,
        out_shape=jax.ShapeDtypeStruct((shards * message, LANES), jnp.bfloat16),
        scratch_shapes=[
            pltpu.VMEM((padded, tokens), jnp.bfloat16),
            pltpu.VMEM((width, LANES), jnp.float32),
        ],
        compiler_params=pltpu.CompilerParams(vmem_limit_bytes=VMEM_LIMIT),
    )(e, dy, gain, stats, owner, row)


def table_call(got, shards, capacity, width, vocab_dev):
    slots = shards * capacity
    return pl.pallas_call(
        lambda *refs: table_kernel(shards, capacity, *refs),
        grid=(pl.cdiv(vocab_dev, TILE),),
        in_specs=[pl.BlockSpec(memory_space=pltpu.VMEM)],
        out_specs=[pl.BlockSpec((width, TILE), lambda j: (0, j)), pl.BlockSpec((1, width), lambda j: (0, 0))],
        out_shape=[
            jax.ShapeDtypeStruct((width, vocab_dev), jnp.bfloat16),
            jax.ShapeDtypeStruct((1, width), jnp.float32),
        ],
        scratch_shapes=[pltpu.VMEM((width, slots), jnp.bfloat16), pltpu.VMEM((slots, LANES), jnp.float32)],
        compiler_params=pltpu.CompilerParams(vmem_limit_bytes=VMEM_LIMIT),
    )(got)


def on_device(emb_rows, grad_normed, norm_gain, owner_shard, row_in_shard):
    tokens, width = emb_rows.shape
    sections, shards = lax.axis_size("section"), lax.axis_size("dp")
    capacity = 3 * tokens // (2 * shards)
    e, dy = emb_rows.T, grad_normed.T
    gain = norm_gain.reshape(1, width)
    owner, row = owner_shard.reshape(1, tokens), row_in_shard.reshape(1, tokens)
    stats = lax.all_to_all(stats_call(e, dy, gain, sections), "section", 0, 0, tiled=True)
    message = rows_call(e, dy, gain, stats, owner, row, shards, capacity)
    message = message.reshape(shards, -1, LANES)
    side = math.isqrt(shards)
    order = [x * side + (x + k) % side for k in range(side) for x in range(side)]
    got = lax.all_to_all(message, "dp", 0, 0, tiled=True, axis_index_groups=[order])
    table, gain_gradient = table_call(got.reshape(-1, LANES), shards, capacity, width, VOCAB // shards)
    return (table.T, gain_gradient.reshape(width))


def solution(mesh):
    return jax.shard_map(
        on_device,
        mesh=mesh,
        in_specs=(
            P("dp", "section"),
            P("dp", "section"),
            P("section"),
            P("dp", None),
            P("dp", None),
        ),
        out_specs=(P("dp", "section"), P("section")),
        check_vma=False,
    )
```

```python
import math

import jax
import jax.numpy as jnp
from jax import lax
from jax.experimental import pallas as pl
from jax.experimental.pallas import tpu as pltpu
from jax.sharding import PartitionSpec as P

MODEL_WIDTH = 7168
VOCAB = 129280
EPS = 1e-06
LANES = 128
STRIP = 16
HALF = LANES // 2
LEVELS = 240 * 128
SCALE_LANE = HALF + 48
LOADS = 2
VMEM_LIMIT = 40 * 1024 * 1024
FULL_VMEM = 62 * 1024 * 1024
PICK = 16
TILE = 1024


def iota(shape, dim):
    return lax.broadcasted_iota(jnp.int32, shape, dim)


def column_of(row):
    n = row.shape[1]
    return jnp.sum(jnp.where(iota((n, n), 0) == iota((n, n), 1), row, 0.0), axis=1, keepdims=True)


def fold_mask(n, lane_dim):
    shape = (n, LANES) if lane_dim == 1 else (LANES, n)
    lane = iota(shape, lane_dim) - HALF
    feature = iota(shape, 1 - lane_dim)
    hit = feature == lane
    for r in range(1, n // HALF):
        hit = hit | (feature - r * HALF == lane)
    return hit & (lane >= 0)


def row_mask(n):
    offset = iota((8, n), 1) - (iota((8, n), 0) - 1) * HALF
    return (offset >= 0) & (offset < HALF)


def encode(q):
    size = jnp.abs(q)
    binade = jnp.floor(size * (1.0 / 128.0))
    value = 1.0 + (size - binade * 128.0) * (1.0 / 128.0)
    value = value * 2.0**-120
    for bit in (128, 64, 32, 16, 8, 4, 2, 1):
        take = binade >= bit
        binade = jnp.where(take, binade - bit, binade)
        for _ in range(2 if bit == 128 else 1):
            value = jnp.where(take, value * 2.0 ** min(bit, 64), value)
    return jnp.where(q < 0, -value, value)


def decode(code):
    value = jnp.abs(code)
    size = jnp.zeros_like(value)
    for bit in (128, 64, 32, 16, 8, 4, 2, 1):
        take = value >= 2.0 ** (bit - 120)
        size = jnp.where(take, size + bit * 128.0, size)
        for _ in range(2 if bit == 128 else 1):
            value = jnp.where(take, value * 2.0 ** -min(bit, 64), value)
    size = size + (value * 2.0**120 * 128.0 - 128.0)
    return jnp.where(code < 0, -size, size)


def copies_of(pairs, sems, parts):
    out = []
    for p in range(parts):
        group = []
        for n, (source, target) in enumerate(pairs):
            rows = source.shape[0] // parts
            where = pl.ds(p * rows, rows)
            group.append(pltpu.make_async_copy(source.at[where], target.at[where], sems.at[p, n]))
        out.append(group)
    return out


def stats_kernel(e_hbm, dy_hbm, gain_hbm, out_ref, e_ref, dy_ref, gain_ref, sems, gain_sem):
    width, tokens = e_ref.shape
    gain_copy = pltpu.make_async_copy(gain_hbm, gain_ref, gain_sem)
    gain_copy.start()
    copies = copies_of([(e_hbm, e_ref), (dy_hbm, dy_ref)], sems, LOADS)
    for group in copies:
        for copy in group:
            copy.start()
    gain_copy.wait()
    gain = column_of(gain_ref[...])
    sq = jnp.zeros((8, tokens), jnp.float32)
    dot = jnp.zeros((8, tokens), jnp.float32)
    for p, group in enumerate(copies):
        for copy in group:
            copy.wait()
        for k in range(p * width // LOADS, (p + 1) * width // LOADS, STRIP):
            e = e_ref[k : k + STRIP, :].astype(jnp.float32)
            dy = dy_ref[k : k + STRIP, :].astype(jnp.float32)
            ee = e * e
            ed = e * (dy * gain[k : k + STRIP])
            sq = sq + ee[:8] + ee[8:]
            dot = dot + ed[:8] + ed[8:]
    sub = iota((8, LANES), 0)
    halves = []
    for total in (sq, dot):
        total = jnp.sum(total, axis=0, keepdims=True)
        tile = jnp.zeros((8, LANES), jnp.float32)
        for s in range(tokens // LANES):
            tile = jnp.where(sub == s, total[:, s * LANES : (s + 1) * LANES], tile)
        halves.append(tile)
    pair = jnp.concatenate(halves, axis=1)
    out_ref[...] = jnp.broadcast_to(pair[None], out_ref.shape)


def ranks_of(owner, shards):
    tokens = owner.shape[1]
    blocks = tokens // LANES
    marks = (iota((shards, tokens), 0) == owner).astype(jnp.float32)
    stacked = jnp.concatenate([marks[:, b * LANES : (b + 1) * LANES] for b in range(blocks)], axis=0)
    earlier = (iota((LANES, LANES), 0) < iota((LANES, LANES), 1)).astype(jnp.bfloat16)
    before = jnp.dot(stacked.astype(jnp.bfloat16), earlier, preferred_element_type=jnp.float32)
    totals = jnp.sum(stacked, axis=1, keepdims=True)
    start = jnp.zeros((shards, 1), jnp.float32)
    ranks = []
    for b in range(blocks):
        rows = slice(b * shards, (b + 1) * shards)
        ranks.append(jnp.sum(stacked[rows] * (before[rows] + start), axis=0, keepdims=True))
        start = start + totals[rows]
    rank = jnp.concatenate(ranks, axis=1).astype(jnp.int32)
    return marks, rank


def rows_kernel(shards, capacity, e_ref, dy_ref, gain_ref, stats_ref, owner_ref, row_ref, out_ref, rows_ref, part_ref):
    width, tokens = e_ref.shape
    padded = rows_ref.shape[0]
    owner = owner_ref[...]
    marks, rank = ranks_of(owner, shards)
    side = math.isqrt(shards)
    line = lax.div(owner, side)
    place = lax.rem(line - lax.rem(owner, side) + side, side) * side + lax.rem(owner, side)
    position = place * capacity + rank
    ids = row_ref[...]
    spot = iota((LANES, tokens), 0) - HALF
    id_rows = jnp.zeros((shards, LANES), jnp.float32)
    for part, first in ((ids >> 3, 0), (ids & 7, capacity)):
        id_rows = id_rows + lax.dot_general(
            (marks * part.astype(jnp.float32)).astype(jnp.bfloat16),
            (spot == rank + first).astype(jnp.float32).astype(jnp.bfloat16),
            (((1,), (1,)), ((), ())),
            preferred_element_type=jnp.float32,
        )
    gain = column_of(gain_ref[...])
    pair = jnp.sum(stats_ref[...], axis=0)
    sq = jnp.concatenate([pair[s : s + 1, :LANES] for s in range(8)], axis=1)
    dot = jnp.concatenate([pair[s : s + 1, LANES:] for s in range(8)], axis=1)
    rinv = lax.rsqrt(sq / MODEL_WIDTH + EPS)
    pull = dot * rinv * rinv / MODEL_WIDTH
    for k in range(0, width, STRIP):
        e = e_ref[k : k + STRIP, :].astype(jnp.float32)
        dy = dy_ref[k : k + STRIP, :].astype(jnp.float32)
        rows_ref[k : k + STRIP, :] = ((dy * gain[k : k + STRIP] - e * pull) * rinv).astype(jnp.bfloat16)
        term = dy * (e * rinv)
        part = term[:, :LANES]
        for s in range(1, tokens // LANES):
            part = part + term[:, s * LANES : (s + 1) * LANES]
        part_ref[k : k + STRIP, :] = part
    rows_ref[width:, :] = jnp.zeros((padded - width, tokens), jnp.bfloat16)
    partial = jnp.sum(part_ref[...], axis=1, keepdims=True)
    scale = jnp.maximum(jnp.max(jnp.abs(partial), axis=0, keepdims=True), 1e-30)
    steps = jnp.floor(partial * ((LEVELS - 1) / scale) + 0.5)
    steps = jnp.clip(steps, -(LEVELS - 1.0), LEVELS - 1.0)
    high = jnp.floor(steps * (1.0 / 128.0))
    spots, lines = fold_mask(width, 1), row_mask(width).astype(jnp.float32).astype(jnp.bfloat16)
    fold = jnp.zeros((8, LANES), jnp.float32)
    for part, unit in ((high, 128.0), (steps - high * 128.0, 1.0)):
        spread = jnp.where(spots, part, 0.0).astype(jnp.bfloat16)
        fold = fold + unit * jnp.dot(lines, spread, preferred_element_type=jnp.float32)
    sub, lane = iota((8, LANES), 0), iota((8, LANES), 1)
    extra = jnp.where((sub > 0) & (lane >= HALF), encode(fold), 0.0)
    for n in range(3):
        piece = scale.astype(jnp.bfloat16).astype(jnp.float32)
        extra = jnp.where((sub == 0) & (lane == SCALE_LANE + n), piece, extra)
        scale = scale - piece
    rows = rows_ref[...]
    for first in range(0, shards, PICK):
        half = PICK // 2 * capacity
        pick = jnp.concatenate([onehot_rows(position, first * capacity + h * half, half) for h in range(2)], axis=0)
        got = lax.dot_general(pick, rows, (((1,), (1,)), ((), ())), preferred_element_type=jnp.float32)
        pieces = []
        for n in range(PICK):
            mine = got[n * capacity : (n + 1) * capacity]
            pieces += [mine[:, k : k + LANES] for k in range(0, padded - LANES, LANES)]
            last = mine[:, padded - LANES :]
            place = first + n
            shard = (place % side + place // side) % side * side + place % side
            pieces.append(last[:8] + pltpu.roll(last[16:], HALF, 1))
            pieces.append(last[8:16] + jnp.where(sub == 0, extra + id_rows[shard : shard + 1], extra))
        size = out_ref.shape[0] // shards * PICK
        out_ref[first // PICK * size : (first // PICK + 1) * size] = jnp.concatenate(pieces, axis=0).astype(jnp.bfloat16)


def onehot_rows(position, base, n):
    local = (position - base).astype(jnp.float32).astype(jnp.bfloat16)
    row = iota((n, position.shape[1]), 0).astype(jnp.float32).astype(jnp.bfloat16)
    return jnp.where(row == local, jnp.bfloat16(1), jnp.bfloat16(0))


def table_kernel(shards, capacity, got_ref, table_ref, gain_ref, turned_ref, id_ref):
    width, tile = table_ref.shape
    slots = shards * capacity
    j = pl.program_id(0)

    def sums():
        sub_tile = min(tile, 256)
        for t in range(tile // sub_tile):
            base = (j * tile + t * sub_tile).astype(jnp.float32)
            local = (id_ref[...] - base).astype(jnp.bfloat16)
            parts = []
            for q in range(sub_tile // LANES):
                lane = (iota((slots, LANES), 1) + q * LANES).astype(jnp.float32).astype(jnp.bfloat16)
                parts.append(jnp.where(local == lane, jnp.bfloat16(1), jnp.bfloat16(0)))
            onehot = jnp.concatenate(parts, axis=1)
            table_ref[:, t * sub_tile : (t + 1) * sub_tile] = jnp.dot(
                turned_ref[...], onehot, preferred_element_type=jnp.float32
            ).astype(jnp.bfloat16)

    @pl.when(j == 0)
    def _():
        got = got_ref[...].astype(jnp.float32).reshape(shards, -1, LANES)
        full = width // LANES
        for k in range(full):
            block = got[:, k * capacity : (k + 1) * capacity].reshape(slots, LANES)
            turned_ref[k * LANES : (k + 1) * LANES] = block.astype(jnp.bfloat16).T
        last = got[:, full * capacity :]
        block = jnp.concatenate([last, pltpu.roll(last[:, :8].reshape(shards * 8, LANES), HALF, 1).reshape(shards, 8, LANES)], axis=1)
        turned_ref[full * LANES :] = block.reshape(slots, LANES).astype(jnp.bfloat16).T[:HALF]
        extra = last[:, 8:]
        spot, lane = iota((capacity, LANES), 0), iota((capacity, LANES), 1) - HALF
        weight = jnp.where(lane == spot, 8.0, jnp.where(lane == spot + capacity, 1.0, 0.0))
        ids = jnp.sum(extra[:, :1] * weight[None], axis=2, keepdims=True).reshape(slots, 1)
        id_ref[...] = jnp.broadcast_to(ids, id_ref.shape)
        sums()
        at = iota((1, LANES), 1)
        scale = jnp.where((at >= SCALE_LANE) & (at < SCALE_LANE + 3), extra[:, 0], 0.0)
        scale = jnp.sum(scale, axis=1, keepdims=True) * (1.0 / (LEVELS - 1))
        fold = jnp.sum(decode(extra) * scale[:, :, None], axis=0)
        spread = jnp.dot(
            fold, fold_mask(width, 0).astype(jnp.float32),
            precision=lax.Precision.HIGHEST, preferred_element_type=jnp.float32,
        )
        gain_ref[...] = jnp.sum(jnp.where(row_mask(width), spread, 0.0), axis=0, keepdims=True)

    @pl.when(j > 0)
    def _():
        sums()


def stats_call(e, dy, gain, sections):
    width, tokens = e.shape
    return pl.pallas_call(
        stats_kernel,
        in_specs=[pl.BlockSpec(memory_space=pltpu.HBM)] * 3,
        out_shape=pltpu.VMEM((sections, 8, 2 * LANES), jnp.float32),
        scratch_shapes=[
            pltpu.VMEM((width, tokens), e.dtype),
            pltpu.VMEM((width, tokens), dy.dtype),
            pltpu.VMEM((1, width), jnp.float32),
            pltpu.SemaphoreType.DMA((LOADS, 2)),
            pltpu.SemaphoreType.DMA,
        ],
        compiler_params=pltpu.CompilerParams(vmem_limit_bytes=FULL_VMEM),
    )(e, dy, gain)


def rows_call(e, dy, gain, stats, owner, row, shards, capacity):
    width, tokens = e.shape
    padded = -(-width // LANES) * LANES
    message = width // LANES * capacity + 16
    return pl.pallas_call(
        lambda *refs: rows_kernel(shards, capacity, *refs),
        in_specs=[pl.BlockSpec(memory_space=pltpu.VMEM)] * 6,
        out_shape=jax.ShapeDtypeStruct((shards * message, LANES), jnp.bfloat16),
        scratch_shapes=[
            pltpu.VMEM((padded, tokens), jnp.bfloat16),
            pltpu.VMEM((width, LANES), jnp.float32),
        ],
        compiler_params=pltpu.CompilerParams(vmem_limit_bytes=VMEM_LIMIT),
    )(e, dy, gain, stats, owner, row)


def table_call(got, shards, capacity, width, vocab_dev):
    slots = shards * capacity
    return pl.pallas_call(
        lambda *refs: table_kernel(shards, capacity, *refs),
        grid=(pl.cdiv(vocab_dev, TILE),),
        in_specs=[pl.BlockSpec(memory_space=pltpu.VMEM)],
        out_specs=[pl.BlockSpec((width, TILE), lambda j: (0, j)), pl.BlockSpec((1, width), lambda j: (0, 0))],
        out_shape=[
            jax.ShapeDtypeStruct((width, vocab_dev), jnp.bfloat16),
            jax.ShapeDtypeStruct((1, width), jnp.float32),
        ],
        scratch_shapes=[pltpu.VMEM((width, slots), jnp.bfloat16), pltpu.VMEM((slots, LANES), jnp.float32)],
        compiler_params=pltpu.CompilerParams(vmem_limit_bytes=VMEM_LIMIT),
    )(got)


def on_device(emb_rows, grad_normed, norm_gain, owner_shard, row_in_shard):
    tokens, width = emb_rows.shape
    sections, shards = lax.axis_size("section"), lax.axis_size("dp")
    capacity = 3 * tokens // (2 * shards)
    e, dy = emb_rows.T, grad_normed.T
    gain = norm_gain.reshape(1, width)
    owner, row = owner_shard.reshape(1, tokens), row_in_shard.reshape(1, tokens)
    stats = lax.all_to_all(stats_call(e, dy, gain, sections), "section", 0, 0, tiled=True)
    message = rows_call(e, dy, gain, stats, owner, row, shards, capacity)
    message = message.reshape(shards, -1, LANES)
    side = math.isqrt(shards)
    order = [(z + k) % side * side + z for k in range(side) for z in range(side)]
    got = lax.all_to_all(message, "dp", 0, 0, tiled=True, axis_index_groups=[order])
    table, gain_gradient = table_call(got.reshape(-1, LANES), shards, capacity, width, VOCAB // shards)
    return (table.T, gain_gradient.reshape(width))


def solution(mesh):
    return jax.shard_map(
        on_device,
        mesh=mesh,
        in_specs=(
            P("dp", "section"),
            P("dp", "section"),
            P("section"),
            P("dp", None),
            P("dp", None),
        ),
        out_specs=(P("dp", "section"), P("section")),
        check_vma=False,
    )
```
